512 devices in a mesh: seq: 512 (over y, z, x, core).
Axes of the slice: x: 4, y: 4, z: 16, core: 2. Of those that a mesh axis runs over, the one named last changes fastest.
Arguments:
- inputs: bfloat16 [65536, 768], P('seq'), may hold values from -6 to 6
- first_norm_gain: float32 [768], replicated, may hold values from 0.5 to 2
- first_kernel_weights: bfloat16 [3, 768, 768], replicated, may hold values from -0.125 to 0.125
- first_expand_weight: bfloat16 [768, 768], replicated, may hold values from -0.21875 to 0.21875
- first_project_weight: bfloat16 [768, 768], replicated, may hold values from -0.21875 to 0.21875
- second_norm_gain: float32 [768], replicated, may hold values from 0.5 to 2
- second_kernel_weights: bfloat16 [3, 768, 768], replicated, may hold values from -0.125 to 0.125
- second_expand_weight: bfloat16 [768, 768], replicated, may hold values from -0.21875 to 0.21875
- second_project_weight: bfloat16 [768, 768], replicated, may hold values from -0.21875 to 0.21875
- cotangent: bfloat16 [65536, 768], P('seq'), may hold values from -6 to 6
Outputs:
- outputs: bfloat16 [65536, 768], P('seq')
- input_gradient_rows: bfloat16 [65536, 768], P('seq')
The draws below stay inside these ranges and needn't reach their ends.
All inputs are finite; a program needn't handle non-finite values.
Results may differ from the reference program's by a relative error of at most 0.02.
Values may be sent and summed in bfloat16 or wider, within the bound.
A program may use at most 64 MiB of HBM per device.

```python
import math
import jax
import jax.numpy as jnp
from jax import lax

C = 768
SPAN = 65536
DILATION_FIRST = 256
DILATION_SECOND = 4096


def levels(own_key, extent, split, low, high):
    factor_of, own = 1.0, jax.random.fold_in(own_key, 6)
    for position, parts in split:
        steps = jnp.exp(jax.random.uniform(jax.random.fold_in(own, position), (parts,), jnp.float32, low / len(split), high / len(split)))
        factor_of = factor_of * jnp.repeat(steps, extent[position] // parts).reshape([-1 if axis == position else 1 for axis in range(len(extent))])
    return factor_of


def normal_values(own_key, dims, spread, limit, split=(), held_as=jnp.bfloat16):
    values = jax.random.normal(own_key, dims, jnp.float32) * spread
    if len(split) > 0:
        values = levels(own_key, dims, split, -0.22, 0.18) * values
    return jnp.clip(values, min=-limit, max=limit).astype(held_as)


def setup_inputs(seed: int = 0) -> dict:
    key_of = jax.random.split(jax.random.key(seed), 11)
    return {
        "inputs": normal_values(key_of[0], (SPAN, C), 1.0, 6.0, ((0, 512),)),
        "first_norm_gain": jnp.clip(jnp.exp(jax.random.uniform(key_of[1], (C,), jnp.float32, math.log(0.5), math.log(2.0))), 0.5, 2.0),
        "first_kernel_weights": normal_values(key_of[2], (3, C, C), (3 * C) ** -0.5, 0.125),
        "first_expand_weight": normal_values(key_of[3], (C, C), C ** -0.5, 0.21875),
        "first_project_weight": normal_values(key_of[4], (C, C), C ** -0.5, 0.21875),
        "second_norm_gain": jnp.clip(jnp.exp(jax.random.uniform(key_of[5], (C,), jnp.float32, math.log(0.5), math.log(2.0))), 0.5, 2.0),
        "second_kernel_weights": normal_values(key_of[6], (3, C, C), (3 * C) ** -0.5, 0.125),
        "second_expand_weight": normal_values(key_of[7], (C, C), C ** -0.5, 0.21875),
        "second_project_weight": normal_values(key_of[8], (C, C), C ** -0.5, 0.21875),
        "cotangent": normal_values(key_of[9], (SPAN, C), 1.0, 6.0, ((0, 512),)),
    }


def displace(values, steps):
    zeros = jnp.zeros((abs(steps), values.shape[1]), values.dtype)
    if steps > 0:
        return jnp.concatenate([zeros, values[:-steps]], axis=0)
    return jnp.concatenate([values[-steps:], zeros], axis=0)

def gelu_back(point, grad):
    return jax.vjp(jax.nn.gelu, point)[1](grad)[0]

def residual_block_forward(inputs, gain, taps, w_mid, w_out, dilation):
    wide = inputs.astype(jnp.float32)
    inv = jax.lax.rsqrt(lax.optimization_barrier(jnp.mean(wide * wide, axis=-1, keepdims=True)) + 1e-06)
    normed = (wide * inv * gain).astype(jnp.bfloat16)
    pre = jnp.dot(displace(normed, dilation), taps[0], preferred_element_type=jnp.float32)
    pre = pre + jnp.dot(normed, taps[1], preferred_element_type=jnp.float32)
    pre = pre + jnp.dot(displace(normed, -dilation), taps[2], preferred_element_type=jnp.float32)
    act = jax.nn.gelu(pre).astype(jnp.bfloat16)
    mid = jnp.dot(act, w_mid, preferred_element_type=jnp.float32)
    hid = jax.nn.gelu(mid).astype(jnp.bfloat16)
    result = (wide + jnp.dot(hid, w_out, preferred_element_type=jnp.float32)).astype(jnp.bfloat16)
    return (result, (wide, inv, pre, mid))

def residual_block_backward(grad_out, saved, gain, taps, w_mid, w_out, dilation):
    wide, inv, pre, mid = saved
    grad_hid = jnp.dot(grad_out, w_out.T, preferred_element_type=jnp.float32)
    grad_mid = gelu_back(mid, grad_hid).astype(jnp.bfloat16)
    grad_act = jnp.dot(grad_mid, w_mid.T, preferred_element_type=jnp.float32)
    grad_pre = gelu_back(pre, grad_act).astype(jnp.bfloat16)
    grad_norm = jnp.dot(grad_pre, taps[1].T, preferred_element_type=jnp.float32)
    grad_norm = grad_norm + displace(jnp.dot(grad_pre, taps[0].T, preferred_element_type=jnp.float32), -dilation)
    grad_norm = grad_norm + displace(jnp.dot(grad_pre, taps[2].T, preferred_element_type=jnp.float32), dilation)
    scaled = gain * grad_norm
    back = inv * scaled - wide * inv ** 3 * lax.optimization_barrier(jnp.mean(wide * scaled, axis=-1, keepdims=True))
    return (grad_out.astype(jnp.float32) + back).astype(jnp.bfloat16)

def reference(inputs, first_norm_gain, first_kernel_weights, first_expand_weight, first_project_weight, second_norm_gain, second_kernel_weights, second_expand_weight, second_project_weight, cotangent):
    leading_block, first_block_residuals = residual_block_forward(inputs, first_norm_gain, first_kernel_weights, first_expand_weight, first_project_weight, DILATION_FIRST)
    outputs, second_block_residuals = residual_block_forward(leading_block, second_norm_gain, second_kernel_weights, second_expand_weight, second_project_weight, DILATION_SECOND)
    leading_block_gradient = residual_block_backward(cotangent, second_block_residuals, second_norm_gain, second_kernel_weights, second_expand_weight, second_project_weight, DILATION_SECOND)
    input_gradient_rows = residual_block_backward(leading_block_gradient, first_block_residuals, first_norm_gain, first_kernel_weights, first_expand_weight, first_project_weight, DILATION_FIRST)
    return (outputs, input_gradient_rows)
```

```python
import math

import jax
import jax.numpy as jnp
from jax import lax
from jax.experimental import pallas as pl
from jax.experimental.pallas import tpu as pltpu
from jax.sharding import PartitionSpec as P

MESH = pl.DeviceIdType.MESH
C = 768
EPS = 1e-6
CURVE = math.sqrt(2.0 / math.pi)
CUBIC = 0.044715

TAPS = (0, 5)
EXPAND = (3, 8)
PROJECT = (4, 9)

NEAR_FWD, FAR_FWD, FAR_BWD, NEAR_BWD = range(4)


def dot(a, b):
    return jnp.dot(a, b, preferred_element_type=jnp.float32)


def gelu_and_slope(v):
    square = v * v
    t = jnp.tanh(v * (CURVE + (CURVE * CUBIC) * square))
    half = 0.5 + 0.5 * t
    slope = half + (0.5 * v) * (1.0 - t * t) * (CURVE + (3.0 * CURVE * CUBIC) * square)
    return v * half, slope


def make_kernel(devices, near, far, rows, chunks):
    part = rows // chunks
    strides = (near, far, far, near)

    def kernel(
        x_hbm, g1_ref, w1_hbm, m1_hbm, p1_hbm, g2_ref, w2_hbm, m2_hbm, p2_hbm, cot_hbm,
        out_hbm, gin_hbm,
        wts, wts_t, x_v, cot_v, nrm1, nrm2, gp2, gp1, x2, hid2, dy1, out_v, gin_v,
        slope_pre1, slope_mid1, slope_pre2, slope_mid2, own, ghid2, inv1, inv2,
        load_sem, store_sem, send_sem, recv_sem,
    ):
        me = lax.axis_index("seq")
        bufs = (nrm1, nrm2, gp2, gp1)

        def exists(distance):
            return (me + distance >= 0) & (me + distance < devices)

        barrier = pltpu.get_barrier_semaphore()
        partners = (-near, near, -far, far)
        for distance in partners:

            @pl.when(exists(distance))
            def _():
                pl.semaphore_signal(barrier, inc=1, device_id=(me + distance,), device_id_type=MESH)

        def load(i, src, dst):
            return pltpu.make_async_copy(src, dst, load_sem.at[i])

        loads = [load(0, x_hbm, x_v)]
        loads.append(load(1, w1_hbm, wts.at[pl.ds(0, 3)]))
        loads.append(load(2, m1_hbm, wts.at[3]))
        loads.append(load(3, p1_hbm, wts.at[4]))
        loads.append(load(4, cot_hbm, cot_v))
        loads.append(load(5, p2_hbm, wts.at[9]))
        loads.append(load(6, m2_hbm, wts.at[8]))
        loads.append(load(7, w2_hbm, wts.at[pl.ds(5, 3)]))
        for one in loads:
            one.start()

        for stage in range(4):
            for slot, distance in ((0, -strides[stage]), (2, strides[stage])):

                @pl.when(jnp.logical_not(exists(distance)))
                def _():
                    bufs[stage][slot] = jnp.zeros((rows, C), jnp.bfloat16)

        def copies(stage, c):
            stride, buf, at = strides[stage], bufs[stage], span(c)
            for side, (slot, distance) in enumerate(((0, stride), (2, -stride))):
                yield (
                    exists(distance),
                    exists(-distance),
                    pltpu.make_async_remote_copy(
                        src_ref=buf.at[1, at],
                        dst_ref=buf.at[slot, at],
                        send_sem=send_sem.at[stage, side, c],
                        recv_sem=recv_sem.at[stage, side, c],
                        device_id=(me + distance,),
                        device_id_type=MESH,
                    ),
                )

        def span(c):
            return pl.ds(pl.multiple_of(c * part, part), part)

        def send(stage, c):
            for sends, _, copy in copies(stage, c):
                pl.when(sends)(copy.start)

        def receive(stage, c):
            for _, receives, copy in copies(stage, c):
                pl.when(receives)(copy.wait_recv)

        def all_sent(stage):
            def body(c, carry):
                for sends, _, copy in copies(stage, c):
                    pl.when(sends)(copy.wait_send)
                return carry

            lax.fori_loop(0, chunks, body, 0)

        def per_chunk(body):
            def step(c, carry):
                body(c, span(c))
                return carry

            lax.fori_loop(0, chunks, step, 0)

        def transpose(*which):
            for i in which:
                wts_t[i] = wts[i].T

        gain1 = g1_ref[...].reshape(1, C)
        gain2 = g2_ref[...].reshape(1, C)

        def normalize(wide, gain):
            inv = lax.rsqrt(jnp.mean(wide * wide, axis=-1, keepdims=True) + EPS)
            return inv, (wide * inv * gain).astype(jnp.bfloat16)

        loads[0].wait()
        inv, normed = normalize(x_v[...].astype(jnp.float32), gain1)
        inv1[...] = inv
        nrm1[1] = normed
        pl.semaphore_wait(barrier, sum(exists(distance).astype(jnp.int32) for distance in partners))

        def first_send(c, at):
            send(NEAR_FWD, c)

        per_chunk(first_send)
        loads[1].wait()
        own[...] = dot(nrm1[1], wts[1])
        loads[2].wait()
        loads[3].wait()

        def first_forward(c, at):
            receive(NEAR_FWD, c)
            pre = own[at, :] + dot(nrm1[0, at], wts[0]) + dot(nrm1[2, at], wts[2])
            act, slope_pre1[at, :] = gelu_and_slope(pre)
            mid = dot(act.astype(jnp.bfloat16), wts[3])
            hid, slope_mid1[at, :] = gelu_and_slope(mid)
            result = x_v[at, :].astype(jnp.float32) + dot(hid.astype(jnp.bfloat16), wts[4])
            result = result.astype(jnp.bfloat16)
            x2[at, :] = result
            inv, normed = normalize(result.astype(jnp.float32), gain2)
            inv2[at, :] = inv
            nrm2[1, at] = normed
            send(FAR_FWD, c)

        per_chunk(first_forward)

        for i in (4, 5, 6, 7):
            loads[i].wait()
        transpose(9)
        ghid2[...] = dot(cot_v[...], wts_t[9])
        own[...] = dot(nrm2[1], wts[6])
        transpose(8)

        def second_block(c, at):
            receive(FAR_FWD, c)
            pre = own[at, :] + dot(nrm2[0, at], wts[5]) + dot(nrm2[2, at], wts[7])
            act, slope_pre = gelu_and_slope(pre)
            mid = dot(act.astype(jnp.bfloat16), wts[8])
            hid, slope_mid = gelu_and_slope(mid)
            hid2[at, :] = hid.astype(jnp.bfloat16)
            grad_mid = (ghid2[at, :] * slope_mid).astype(jnp.bfloat16)
            grad_act = dot(grad_mid, wts_t[8])
            gp2[1, at] = (grad_act * slope_pre).astype(jnp.bfloat16)
            send(FAR_BWD, c)

            @pl.when(c == 0)
            def _():
                transpose(5, 6, 7)

            @pl.when(c == 1)
            def _():
                transpose(4, 3)

            @pl.when(c == 2)
            def _():
                transpose(0, 1, 2)

        per_chunk(second_block)
        out_v[...] = (x2[...].astype(jnp.float32) + dot(hid2[...], wts[9])).astype(jnp.bfloat16)
        store_out = pltpu.make_async_copy(out_v, out_hbm, store_sem.at[0])
        store_out.start()
        own[...] = dot(gp2[1], wts_t[6])

        def norm_backward(dy, wide, inv, gain, grad_norm):
            scaled = gain * grad_norm
            inner = jnp.mean(wide * scaled, axis=-1, keepdims=True)
            return (dy + (inv * scaled - wide * (inv * inv * inv * inner))).astype(jnp.bfloat16)

        def second_to_first(c, at):
            receive(FAR_BWD, c)
            grad_norm = own[at, :] + dot(gp2[2, at], wts_t[5]) + dot(gp2[0, at], wts_t[7])
            dy = norm_backward(
                cot_v[at, :].astype(jnp.float32), x2[at, :].astype(jnp.float32), inv2[at, :], gain2, grad_norm
            )
            dy1[at, :] = dy
            grad_mid = (dot(dy, wts_t[4]) * slope_mid1[at, :]).astype(jnp.bfloat16)
            gp1[1, at] = (dot(grad_mid, wts_t[3]) * slope_pre1[at, :]).astype(jnp.bfloat16)
            send(NEAR_BWD, c)

        per_chunk(second_to_first)
        own[...] = dot(gp1[1], wts_t[1])

        def first_backward(c, at):
            receive(NEAR_BWD, c)
            grad_norm = own[at, :] + dot(gp1[2, at], wts_t[0]) + dot(gp1[0, at], wts_t[2])
            gin_v[at, :] = norm_backward(
                dy1[at, :].astype(jnp.float32), x_v[at, :].astype(jnp.float32), inv1[at, :], gain1, grad_norm
            )

        per_chunk(first_backward)
        store_gin = pltpu.make_async_copy(gin_v, gin_hbm, store_sem.at[1])
        store_gin.start()
        for stage in range(4):
            all_sent(stage)
        store_out.wait()
        store_gin.wait()

    return kernel


def solution(mesh):
    devices = mesh.shape["seq"]
    chunks = 4

    def per_device(x, g1, w1, m1, p1, g2, w2, m2, p2, cot):
        rows = x.shape[0]
        span = devices * rows
        near, far = 256 // rows, 4096 // rows
        assert span == 65536
        bf16 = lambda *lead: pltpu.VMEM((*lead, rows, C), jnp.bfloat16)
        f32 = lambda: pltpu.VMEM((rows, C), jnp.float32)
        whole = pl.BlockSpec(memory_space=pl.ANY)
        vmem = pl.BlockSpec(memory_space=pltpu.VMEM)
        block = jax.ShapeDtypeStruct((rows, C), jnp.bfloat16)
        results = pl.pallas_call(
            make_kernel(devices, near, far, rows, chunks),
            out_shape=(block, block),
            in_specs=[whole, vmem, whole, whole, whole, vmem, whole, whole, whole, whole],
            out_specs=(whole, whole),
            scratch_shapes=[
                pltpu.VMEM((10, C, C), jnp.bfloat16),
                pltpu.VMEM((10, C, C), jnp.bfloat16),
                bf16(), bf16(), bf16(3), bf16(3), bf16(3), bf16(3), bf16(), bf16(), bf16(), bf16(), bf16(),
                f32(), f32(), f32(), f32(), f32(), f32(),
                pltpu.VMEM((rows, 1), jnp.float32),
                pltpu.VMEM((rows, 1), jnp.float32),
                pltpu.SemaphoreType.DMA((8,)),
                pltpu.SemaphoreType.DMA((2,)),
                pltpu.SemaphoreType.DMA((4, 2, chunks)),
                pltpu.SemaphoreType.DMA((4, 2, chunks)),
            ],
            compiler_params=pltpu.CompilerParams(
                collective_id=0, has_side_effects=True, vmem_limit_bytes=62 << 20
            ),
        )(x, g1, w1, m1, p1, g2, w2, m2, p2, cot)

        def hand_over(a, b, a_out, b_out):
            a_out[...] = a[...]
            b_out[...] = b[...]

        return pl.pallas_call(
            hand_over,
            out_shape=(block, block),
            in_specs=[vmem, vmem],
            out_specs=(vmem, vmem),
            compiler_params=pltpu.CompilerParams(vmem_limit_bytes=62 << 20),
        )(*results)

    return jax.shard_map(
        per_device,
        mesh=mesh,
        in_specs=(P("seq", None), P(), P(), P(), P(), P(), P(), P(), P(), P("seq", None)),
        out_specs=(P("seq", None), P("seq", None)),
        check_vma=False,
    )
```

```python
import math

import jax
import jax.numpy as jnp
from jax import lax
from jax.experimental import pallas as pl
from jax.experimental.pallas import tpu as pltpu
from jax.sharding import PartitionSpec as P

MESH = pl.DeviceIdType.MESH
C = 768
EPS = 1e-6
CURVE = math.sqrt(2.0 / math.pi)
CUBIC = 0.044715

TAPS = (0, 5)
EXPAND = (3, 8)
PROJECT = (4, 9)

NEAR_FWD, FAR_FWD, FAR_BWD, NEAR_BWD = range(4)

DEPTH = {FAR_FWD: 1, FAR_BWD: 1}


def dot(a, b):
    return jnp.dot(a, b, preferred_element_type=jnp.float32)


def gelu_and_slope(v):
    square = v * v
    t = jnp.tanh(v * (CURVE + (CURVE * CUBIC) * square))
    half = 0.5 + 0.5 * t
    slope = half + (0.5 * v) * (1.0 - t * t) * (CURVE + (3.0 * CURVE * CUBIC) * square)
    return v * half, slope


def make_kernel(devices, near, far, rows, chunks):
    part = rows // chunks
    strides = (near, far, far, near)

    def kernel(
        x_hbm, g1_ref, w1_hbm, m1_hbm, p1_hbm, g2_ref, w2_hbm, m2_hbm, p2_hbm, cot_hbm,
        out_hbm, gin_hbm,
        wts, wts_t, x_v, cot_v, nrm1, nrm2, gp2, gp1, x2, hid2, dy1, out_v, gin_v,
        slope_pre1, slope_mid1, slope_pre2, slope_mid2, own, ghid2, inv1, inv2,
        load_sem, store_sem, send_sem, recv_sem,
    ):
        me = lax.axis_index("seq")
        bufs = (nrm1, nrm2, gp2, gp1)

        def exists(distance):
            return (me + distance >= 0) & (me + distance < devices)

        barrier = pltpu.get_barrier_semaphore()
        partners = (-near, near, -far, far)
        for distance in partners:

            @pl.when(exists(distance))
            def _():
                pl.semaphore_signal(barrier, inc=1, device_id=(me + distance,), device_id_type=MESH)

        def load(i, src, dst):
            return pltpu.make_async_copy(src, dst, load_sem.at[i])

        loads = [load(0, x_hbm, x_v)]
        loads.append(load(1, w1_hbm, wts.at[pl.ds(0, 3)]))
        loads.append(load(2, m1_hbm, wts.at[3]))
        loads.append(load(3, p1_hbm, wts.at[4]))
        loads.append(load(4, cot_hbm, cot_v))
        loads.append(load(5, p2_hbm, wts.at[9]))
        loads.append(load(6, m2_hbm, wts.at[8]))
        loads.append(load(7, w2_hbm, wts.at[pl.ds(5, 3)]))
        for one in loads:
            one.start()

        for stage in range(4):
            for slot, distance in ((0, -strides[stage]), (2, strides[stage])):

                @pl.when(jnp.logical_not(exists(distance)))
                def _():
                    bufs[stage][slot] = jnp.zeros((rows, C), jnp.bfloat16)

        def copies(stage, c):
            stride, buf, at = strides[stage], bufs[stage], span(c)
            for side, (slot, distance) in enumerate(((0, stride), (2, -stride))):
                yield (
                    exists(distance),
                    exists(-distance),
                    pltpu.make_async_remote_copy(
                        src_ref=buf.at[1, at],
                        dst_ref=buf.at[slot, at],
                        send_sem=send_sem.at[stage, side, c],
                        recv_sem=recv_sem.at[stage, side, c],
                        device_id=(me + distance,),
                        device_id_type=MESH,
                    ),
                )

        def span(c):
            return pl.ds(pl.multiple_of(c * part, part), part)

        def send(stage, c):
            for sends, _, copy in copies(stage, c):
                pl.when(sends)(copy.start)

        def receive(stage, c):
            for _, receives, copy in copies(stage, c):
                pl.when(receives)(copy.wait_recv)

        def sent(stage, c):
            for sends, _, copy in copies(stage, c):
                pl.when(sends)(copy.wait_send)

        def send_far(stage, c):
            @pl.when(held[stage] & (c >= DEPTH[stage]))
            def _():
                sent(stage, c - DEPTH[stage])

            send(stage, c)

        def all_sent(stage):
            def body(c, carry):
                waited = held[stage] & (c < chunks - DEPTH[stage]) if stage in held else False

                @pl.when(jnp.logical_not(waited))
                def _():
                    sent(stage, c)

                return carry

            lax.fori_loop(0, chunks, body, 0)

        def per_chunk(body):
            def step(c, carry):
                body(c, span(c))
                return carry

            lax.fori_loop(0, chunks, step, 0)

        def transpose(*which):
            for i in which:
                wts_t[i] = wts[i].T

        gain1 = g1_ref[...].reshape(1, C)
        gain2 = g2_ref[...].reshape(1, C)

        def normalize(wide, gain):
            inv = lax.rsqrt(jnp.mean(wide * wide, axis=-1, keepdims=True) + EPS)
            return inv, (wide * inv * gain).astype(jnp.bfloat16)

        lane, slab = lax.rem(me // (far // 4), 4), lax.rem(me // far, 4)
        held = {FAR_FWD: ((lane == 1) | (lane == 2)), FAR_BWD: ((lane == 1) | (lane == 2))}

        loads[0].wait()
        inv, normed = normalize(x_v[...].astype(jnp.float32), gain1)
        inv1[...] = inv
        nrm1[1] = normed
        pl.semaphore_wait(barrier, sum(exists(distance).astype(jnp.int32) for distance in partners))

        def first_send(c, at):
            send(NEAR_FWD, c)

        per_chunk(first_send)
        loads[1].wait()
        own[...] = dot(nrm1[1], wts[1])
        loads[2].wait()
        loads[3].wait()

        def first_forward(c, at):
            receive(NEAR_FWD, c)
            pre = own[at, :] + dot(nrm1[0, at], wts[0]) + dot(nrm1[2, at], wts[2])
            act, slope_pre1[at, :] = gelu_and_slope(pre)
            mid = dot(act.astype(jnp.bfloat16), wts[3])
            hid, slope_mid1[at, :] = gelu_and_slope(mid)
            result = x_v[at, :].astype(jnp.float32) + dot(hid.astype(jnp.bfloat16), wts[4])
            result = result.astype(jnp.bfloat16)
            x2[at, :] = result
            inv, normed = normalize(result.astype(jnp.float32), gain2)
            inv2[at, :] = inv
            nrm2[1, at] = normed
            send_far(FAR_FWD, c)

        per_chunk(first_forward)

        for i in (4, 5, 6, 7):
            loads[i].wait()
        transpose(9)
        ghid2[...] = dot(cot_v[...], wts_t[9])
        own[...] = dot(nrm2[1], wts[6])
        transpose(8)

        def second_block(c, at):
            receive(FAR_FWD, c)
            pre = own[at, :] + dot(nrm2[0, at], wts[5]) + dot(nrm2[2, at], wts[7])
            act, slope_pre = gelu_and_slope(pre)
            mid = dot(act.astype(jnp.bfloat16), wts[8])
            hid, slope_mid = gelu_and_slope(mid)
            hid2[at, :] = hid.astype(jnp.bfloat16)
            grad_mid = (ghid2[at, :] * slope_mid).astype(jnp.bfloat16)
            grad_act = dot(grad_mid, wts_t[8])
            gp2[1, at] = (grad_act * slope_pre).astype(jnp.bfloat16)
            send_far(FAR_BWD, c)

            @pl.when(c == 0)
            def _():
                transpose(5, 6, 7)

            @pl.when(c == 1)
            def _():
                transpose(4, 3)

            @pl.when(c == 2)
            def _():
                transpose(0, 1, 2)

        per_chunk(second_block)
        out_v[...] = (x2[...].astype(jnp.float32) + dot(hid2[...], wts[9])).astype(jnp.bfloat16)
        store_out = pltpu.make_async_copy(out_v, out_hbm, store_sem.at[0])
        store_out.start()
        own[...] = dot(gp2[1], wts_t[6])

        def norm_backward(dy, wide, inv, gain, grad_norm):
            scaled = gain * grad_norm
            inner = jnp.mean(wide * scaled, axis=-1, keepdims=True)
            return (dy + (inv * scaled - wide * (inv * inv * inv * inner))).astype(jnp.bfloat16)

        def second_to_first(c, at):
            receive(FAR_BWD, c)
            grad_norm = own[at, :] + dot(gp2[2, at], wts_t[5]) + dot(gp2[0, at], wts_t[7])
            dy = norm_backward(
                cot_v[at, :].astype(jnp.float32), x2[at, :].astype(jnp.float32), inv2[at, :], gain2, grad_norm
            )
            dy1[at, :] = dy
            grad_mid = (dot(dy, wts_t[4]) * slope_mid1[at, :]).astype(jnp.bfloat16)
            gp1[1, at] = (dot(grad_mid, wts_t[3]) * slope_pre1[at, :]).astype(jnp.bfloat16)
            send(NEAR_BWD, c)

        per_chunk(second_to_first)
        own[...] = dot(gp1[1], wts_t[1])

        def first_backward(c, at):
            receive(NEAR_BWD, c)
            grad_norm = own[at, :] + dot(gp1[2, at], wts_t[0]) + dot(gp1[0, at], wts_t[2])
            gin_v[at, :] = norm_backward(
                dy1[at, :].astype(jnp.float32), x_v[at, :].astype(jnp.float32), inv1[at, :], gain1, grad_norm
            )

        per_chunk(first_backward)
        store_gin = pltpu.make_async_copy(gin_v, gin_hbm, store_sem.at[1])
        store_gin.start()
        for stage in range(4):
            all_sent(stage)
        store_out.wait()
        store_gin.wait()

    return kernel


def solution(mesh):
    devices = mesh.shape["seq"]
    chunks = 4

    def per_device(x, g1, w1, m1, p1, g2, w2, m2, p2, cot):
        rows = x.shape[0]
        span = devices * rows
        near, far = 256 // rows, 4096 // rows
        assert span == 65536
        bf16 = lambda *lead: pltpu.VMEM((*lead, rows, C), jnp.bfloat16)
        f32 = lambda: pltpu.VMEM((rows, C), jnp.float32)
        whole = pl.BlockSpec(memory_space=pl.ANY)
        vmem = pl.BlockSpec(memory_space=pltpu.VMEM)
        block = jax.ShapeDtypeStruct((rows, C), jnp.bfloat16)
        results = pl.pallas_call(
            make_kernel(devices, near, far, rows, chunks),
            out_shape=(block, block),
            in_specs=[whole, vmem, whole, whole, whole, vmem, whole, whole, whole, whole],
            out_specs=(whole, whole),
            scratch_shapes=[
                pltpu.VMEM((10, C, C), jnp.bfloat16),
                pltpu.VMEM((10, C, C), jnp.bfloat16),
                bf16(), bf16(), bf16(3), bf16(3), bf16(3), bf16(3), bf16(), bf16(), bf16(), bf16(), bf16(),
                f32(), f32(), f32(), f32(), f32(), f32(),
                pltpu.VMEM((rows, 1), jnp.float32),
                pltpu.VMEM((rows, 1), jnp.float32),
                pltpu.SemaphoreType.DMA((8,)),
                pltpu.SemaphoreType.DMA((2,)),
                pltpu.SemaphoreType.DMA((4, 2, chunks)),
                pltpu.SemaphoreType.DMA((4, 2, chunks)),
            ],
            compiler_params=pltpu.CompilerParams(
                collective_id=0, has_side_effects=True, vmem_limit_bytes=62 << 20
            ),
        )(x, g1, w1, m1, p1, g2, w2, m2, p2, cot)

        def hand_over(a, b, a_out, b_out):
            a_out[...] = a[...]
            b_out[...] = b[...]

        return pl.pallas_call(
            hand_over,
            out_shape=(block, block),
            in_specs=[vmem, vmem],
            out_specs=(vmem, vmem),
            compiler_params=pltpu.CompilerParams(vmem_limit_bytes=62 << 20),
        )(*results)

    return jax.shard_map(
        per_device,
        mesh=mesh,
        in_specs=(P("seq", None), P(), P(), P(), P(), P(), P(), P(), P(), P("seq", None)),
        out_specs=(P("seq", None), P("seq", None)),
        check_vma=False,
    )
```

```python
import math

import jax
import jax.numpy as jnp
from jax import lax
from jax.experimental import pallas as pl
from jax.experimental.pallas import tpu as pltpu
from jax.sharding import PartitionSpec as P

MESH = pl.DeviceIdType.MESH
C = 768
EPS = 1e-6
CURVE = math.sqrt(2.0 / math.pi)
CUBIC = 0.044715

TAPS = (0, 5)
EXPAND = (3, 8)
PROJECT = (4, 9)

NEAR_FWD, FAR_FWD, FAR_BWD, NEAR_BWD = range(4)

DEPTH = {FAR_FWD: 1, FAR_BWD: 1}


def dot(a, b):
    return jnp.dot(a, b, preferred_element_type=jnp.float32)


def gelu_and_slope(v):
    square = v * v
    t = jnp.tanh(v * (CURVE + (CURVE * CUBIC) * square))
    half = 0.5 + 0.5 * t
    slope = half + (0.5 * v) * (1.0 - t * t) * (CURVE + (3.0 * CURVE * CUBIC) * square)
    return v * half, slope


def make_kernel(devices, near, far, rows, chunks):
    part = rows // chunks
    strides = (near, far, far, near)

    def kernel(
        x_hbm, g1_hbm, w1_hbm, m1_hbm, p1_hbm, g2_hbm, w2_hbm, m2_hbm, p2_hbm, cot_hbm,
        out_hbm, gin_hbm,
        wts, wts_t, x_v, cot_v, nrm1, nrm2, gp2, gp1, x2, hid2, dy1, out_v, gin_v,
        slope_pre1, slope_mid1, slope_pre2, slope_mid2, own, ghid2, inv1, inv2, g1_ref, g2_ref,
        load_sem, store_sem, send_sem, recv_sem,
    ):
        me = lax.axis_index("seq")
        bufs = (nrm1, nrm2, gp2, gp1)

        def exists(distance):
            return (me + distance >= 0) & (me + distance < devices)

        barrier = pltpu.get_barrier_semaphore()
        partners = (-near, near, -far, far)
        for distance in partners:

            @pl.when(exists(distance))
            def _():
                pl.semaphore_signal(barrier, inc=1, device_id=(me + distance,), device_id_type=MESH)

        def load(i, src, dst):
            return pltpu.make_async_copy(src, dst, load_sem.at[i])

        loads = [load(0, x_hbm, x_v)]
        gains = [load(8, g1_hbm, g1_ref), load(9, g2_hbm, g2_ref)]
        loads.append(load(1, w1_hbm, wts.at[pl.ds(0, 3)]))
        loads.append(load(2, m1_hbm, wts.at[3]))
        loads.append(load(3, p1_hbm, wts.at[4]))
        loads.append(load(4, cot_hbm, cot_v))
        loads.append(load(5, p2_hbm, wts.at[9]))
        loads.append(load(6, m2_hbm, wts.at[8]))
        loads.append(load(7, w2_hbm, wts.at[pl.ds(5, 3)]))
        for one in gains + loads:
            one.start()

        for stage in range(4):
            for slot, distance in ((0, -strides[stage]), (2, strides[stage])):

                @pl.when(jnp.logical_not(exists(distance)))
                def _():
                    bufs[stage][slot] = jnp.zeros((rows, C), jnp.bfloat16)

        def copies(stage, c):
            stride, buf, at = strides[stage], bufs[stage], span(c)
            for side, (slot, distance) in enumerate(((0, stride), (2, -stride))):
                yield (
                    exists(distance),
                    exists(-distance),
                    pltpu.make_async_remote_copy(
                        src_ref=buf.at[1, at],
                        dst_ref=buf.at[slot, at],
                        send_sem=send_sem.at[stage, side, c],
                        recv_sem=recv_sem.at[stage, side, c],
                        device_id=(me + distance,),
                        device_id_type=MESH,
                    ),
                )

        def span(c):
            return pl.ds(pl.multiple_of(c * part, part), part)

        def send(stage, c):
            for sends, _, copy in copies(stage, c):
                pl.when(sends)(copy.start)

        def receive(stage, c):
            for _, receives, copy in copies(stage, c):
                pl.when(receives)(copy.wait_recv)

        def sent(stage, c):
            for sends, _, copy in copies(stage, c):
                pl.when(sends)(copy.wait_send)

        def send_far(stage, c):
            @pl.when(held[stage] & (c >= DEPTH[stage]))
            def _():
                sent(stage, c - DEPTH[stage])

            send(stage, c)

        def all_sent(stage):
            def body(c, carry):
                waited = held[stage] & (c < chunks - DEPTH[stage]) if stage in held else False

                @pl.when(jnp.logical_not(waited))
                def _():
                    sent(stage, c)

                return carry

            lax.fori_loop(0, chunks, body, 0)

        def per_chunk(body):
            def step(c, carry):
                body(c, span(c))
                return carry

            lax.fori_loop(0, chunks, step, 0)

        def transpose(*which):
            for i in which:
                wts_t[i] = wts[i].T


        def normalize(wide, gain):
            inv = lax.rsqrt(jnp.mean(wide * wide, axis=-1, keepdims=True) + EPS)
            return inv, (wide * inv * gain).astype(jnp.bfloat16)

        lane, slab = lax.rem(me // (far // 4), 4), lax.rem(me // far, 4)
        held = {FAR_FWD: ((lane == 1) | (lane == 2)), FAR_BWD: ((lane == 1) | (lane == 2)) | (lax.rem(me, 2) == 1)}

        for one in gains + loads[:1]:
            one.wait()
        gain1 = g1_ref[...].reshape(1, C)
        gain2 = g2_ref[...].reshape(1, C)
        inv, normed = normalize(x_v[...].astype(jnp.float32), gain1)
        inv1[...] = inv
        nrm1[1] = normed
        pl.semaphore_wait(barrier, sum(exists(distance).astype(jnp.int32) for distance in partners))

        def first_send(c, at):
            send(NEAR_FWD, c)

        per_chunk(first_send)
        loads[1].wait()
        own[...] = dot(nrm1[1], wts[1])
        loads[2].wait()
        loads[3].wait()

        def first_forward(c, at):
            receive(NEAR_FWD, c)
            pre = own[at, :] + dot(nrm1[0, at], wts[0]) + dot(nrm1[2, at], wts[2])
            act, slope_pre1[at, :] = gelu_and_slope(pre)
            mid = dot(act.astype(jnp.bfloat16), wts[3])
            hid, slope_mid1[at, :] = gelu_and_slope(mid)
            result = x_v[at, :].astype(jnp.float32) + dot(hid.astype(jnp.bfloat16), wts[4])
            result = result.astype(jnp.bfloat16)
            x2[at, :] = result
            inv, normed = normalize(result.astype(jnp.float32), gain2)
            inv2[at, :] = inv
            nrm2[1, at] = normed
            send_far(FAR_FWD, c)

        per_chunk(first_forward)

        for i in (4, 5, 6, 7):
            loads[i].wait()
        transpose(9)
        ghid2[...] = dot(cot_v[...], wts_t[9])
        own[...] = dot(nrm2[1], wts[6])
        transpose(8)

        def second_block(c, at):
            receive(FAR_FWD, c)
            pre = own[at, :] + dot(nrm2[0, at], wts[5]) + dot(nrm2[2, at], wts[7])
            act, slope_pre = gelu_and_slope(pre)
            mid = dot(act.astype(jnp.bfloat16), wts[8])
            hid, slope_mid = gelu_and_slope(mid)
            hid2[at, :] = hid.astype(jnp.bfloat16)
            grad_mid = (ghid2[at, :] * slope_mid).astype(jnp.bfloat16)
            grad_act = dot(grad_mid, wts_t[8])
            gp2[1, at] = (grad_act * slope_pre).astype(jnp.bfloat16)
            send_far(FAR_BWD, c)

            @pl.when(c == 0)
            def _():
                transpose(5, 6, 7)

            @pl.when(c == 1)
            def _():
                transpose(4, 3)

            @pl.when(c == 2)
            def _():
                transpose(0, 1, 2)

        per_chunk(second_block)
        out_v[...] = (x2[...].astype(jnp.float32) + dot(hid2[...], wts[9])).astype(jnp.bfloat16)
        store_out = pltpu.make_async_copy(out_v, out_hbm, store_sem.at[0])
        store_out.start()
        own[...] = dot(gp2[1], wts_t[6])

        def norm_backward(dy, wide, inv, gain, grad_norm):
            scaled = gain * grad_norm
            inner = jnp.mean(wide * scaled, axis=-1, keepdims=True)
            return (dy + (inv * scaled - wide * (inv * inv * inv * inner))).astype(jnp.bfloat16)

        def second_to_first(c, at):
            receive(FAR_BWD, c)
            grad_norm = own[at, :] + dot(gp2[2, at], wts_t[5]) + dot(gp2[0, at], wts_t[7])
            dy = norm_backward(
                cot_v[at, :].astype(jnp.float32), x2[at, :].astype(jnp.float32), inv2[at, :], gain2, grad_norm
            )
            dy1[at, :] = dy
            grad_mid = (dot(dy, wts_t[4]) * slope_mid1[at, :]).astype(jnp.bfloat16)
            gp1[1, at] = (dot(grad_mid, wts_t[3]) * slope_pre1[at, :]).astype(jnp.bfloat16)
            send(NEAR_BWD, c)

        per_chunk(second_to_first)
        own[...] = dot(gp1[1], wts_t[1])

        def first_backward(c, at):
            receive(NEAR_BWD, c)
            grad_norm = own[at, :] + dot(gp1[2, at], wts_t[0]) + dot(gp1[0, at], wts_t[2])
            gin_v[at, :] = norm_backward(
                dy1[at, :].astype(jnp.float32), x_v[at, :].astype(jnp.float32), inv1[at, :], gain1, grad_norm
            )

        per_chunk(first_backward)
        store_gin = pltpu.make_async_copy(gin_v, gin_hbm, store_sem.at[1])
        store_gin.start()
        for stage in range(4):
            all_sent(stage)
        store_out.wait()
        store_gin.wait()

    return kernel


def solution(mesh):
    devices = mesh.shape["seq"]
    chunks = 4

    def per_device(x, g1, w1, m1, p1, g2, w2, m2, p2, cot):
        rows = x.shape[0]
        span = devices * rows
        near, far = 256 // rows, 4096 // rows
        assert span == 65536
        bf16 = lambda *lead: pltpu.VMEM((*lead, rows, C), jnp.bfloat16)
        f32 = lambda: pltpu.VMEM((rows, C), jnp.float32)
        whole = pl.BlockSpec(memory_space=pl.ANY)
        vmem = pl.BlockSpec(memory_space=pltpu.VMEM)
        block = jax.ShapeDtypeStruct((rows, C), jnp.bfloat16)
        results = pl.pallas_call(
            make_kernel(devices, near, far, rows, chunks),
            out_shape=(block, block),
            in_specs=[whole] * 10,
            out_specs=(whole, whole),
            scratch_shapes=[
                pltpu.VMEM((10, C, C), jnp.bfloat16),
                pltpu.VMEM((10, C, C), jnp.bfloat16),
                bf16(), bf16(), bf16(3), bf16(3), bf16(3), bf16(3), bf16(), bf16(), bf16(), bf16(), bf16(),
                f32(), f32(), f32(), f32(), f32(), f32(),
                pltpu.VMEM((rows, 1), jnp.float32),
                pltpu.VMEM((rows, 1), jnp.float32),
                pltpu.VMEM((C,), jnp.float32),
                pltpu.VMEM((C,), jnp.float32),
                pltpu.SemaphoreType.DMA((10,)),
                pltpu.SemaphoreType.DMA((2,)),
                pltpu.SemaphoreType.DMA((4, 2, chunks)),
                pltpu.SemaphoreType.DMA((4, 2, chunks)),
            ],
            compiler_params=pltpu.CompilerParams(
                collective_id=0, has_side_effects=True, vmem_limit_bytes=62 << 20
            ),
        )(x, g1, w1, m1, p1, g2, w2, m2, p2, cot)

        def hand_over(a, b, a_out, b_out):
            a_out[...] = a[...]
            b_out[...] = b[...]

        return pl.pallas_call(
            hand_over,
            out_shape=(block, block),
            in_specs=[vmem, vmem],
            out_specs=(vmem, vmem),
            compiler_params=pltpu.CompilerParams(vmem_limit_bytes=62 << 20),
        )(*results)

    return jax.shard_map(
        per_device,
        mesh=mesh,
        in_specs=(P("seq", None), P(), P(), P(), P(), P(), P(), P(), P(), P("seq", None)),
        out_specs=(P("seq", None), P("seq", None)),
        check_vma=False,
    )
```

```python
import math

import jax
import jax.numpy as jnp
from jax import lax
from jax.experimental import pallas as pl
from jax.experimental.pallas import tpu as pltpu
from jax.sharding import PartitionSpec as P

MESH = pl.DeviceIdType.MESH
C = 768
EPS = 1e-6
CURVE = math.sqrt(2.0 / math.pi)
CUBIC = 0.044715

TAPS = (0, 5)
EXPAND = (3, 8)
PROJECT = (4, 9)

NEAR_FWD, FAR_FWD, FAR_BWD, NEAR_BWD = range(4)

DEPTH = {FAR_FWD: 1, FAR_BWD: 1}


def dot(a, b):
    return jnp.dot(a, b, preferred_element_type=jnp.float32)


def gelu_and_slope(v):
    square = v * v
    t = jnp.tanh(v * (CURVE + (CURVE * CUBIC) * square))
    half = 0.5 + 0.5 * t
    slope = half + (0.5 * v) * (1.0 - t * t) * (CURVE + (3.0 * CURVE * CUBIC) * square)
    return v * half, slope


def make_kernel(devices, near, far, rows, chunks):
    part = rows // chunks
    strides = (near, far, far, near)

    def kernel(
        x_hbm, g1_hbm, w1_hbm, m1_hbm, p1_hbm, g2_hbm, w2_hbm, m2_hbm, p2_hbm, cot_hbm,
        out_hbm, gin_hbm,
        wts, wts_t, x_v, cot_v, nrm1, nrm2, gp2, gp1, x2, hid2, dy1, out_v, gin_v,
        slope_pre1, slope_mid1, slope_pre2, slope_mid2, own, ghid2, inv1, inv2, g1_ref, g2_ref,
        load_sem, store_sem, send_sem, recv_sem,
    ):
        me = lax.axis_index("seq")
        bufs = (nrm1, nrm2, gp2, gp1)

        def exists(distance):
            return (me + distance >= 0) & (me + distance < devices)

        def load(i, src, dst):
            return pltpu.make_async_copy(src, dst, load_sem.at[i])

        loads = [load(0, x_hbm, x_v)]
        gains = [load(8, g1_hbm, g1_ref), load(9, g2_hbm, g2_ref)]
        loads.append(load(1, w1_hbm, wts.at[pl.ds(0, 3)]))
        loads.append(load(2, m1_hbm, wts.at[3]))
        loads.append(load(3, p1_hbm, wts.at[4]))
        loads.append(load(4, cot_hbm, cot_v))
        loads.append(load(5, p2_hbm, wts.at[9]))
        loads.append(load(6, m2_hbm, wts.at[8]))
        loads.append(load(7, w2_hbm, wts.at[pl.ds(5, 3)]))
        for one in loads[:1] + gains:
            one.start()

        barrier = pltpu.get_barrier_semaphore()
        partners = (-near, near, -far, far)
        for distance in partners:

            @pl.when(exists(distance))
            def _():
                pl.semaphore_signal(barrier, inc=1, device_id=(me + distance,), device_id_type=MESH)

        for one in loads[1:]:
            one.start()

        for stage in range(4):
            for slot, distance in ((0, -strides[stage]), (2, strides[stage])):

                @pl.when(jnp.logical_not(exists(distance)))
                def _():
                    bufs[stage][slot] = jnp.zeros((rows, C), jnp.bfloat16)

        def copies(stage, c):
            stride, buf, at = strides[stage], bufs[stage], span(c)
            for side, (slot, distance) in enumerate(((0, stride), (2, -stride))):
                yield (
                    exists(distance),
                    exists(-distance),
                    pltpu.make_async_remote_copy(
                        src_ref=buf.at[1, at],
                        dst_ref=buf.at[slot, at],
                        send_sem=send_sem.at[stage, side, c],
                        recv_sem=recv_sem.at[stage, side, c],
                        device_id=(me + distance,),
                        device_id_type=MESH,
                    ),
                )

        def span(c):
            return pl.ds(pl.multiple_of(c * part, part), part)

        def send(stage, c):
            for sends, _, copy in copies(stage, c):
                pl.when(sends)(copy.start)

        def receive(stage, c):
            for _, receives, copy in copies(stage, c):
                pl.when(receives)(copy.wait_recv)

        def sent(stage, c):
            for sends, _, copy in copies(stage, c):
                pl.when(sends)(copy.wait_send)

        def send_far(stage, c):
            @pl.when(held[stage] & (c >= DEPTH[stage]))
            def _():
                sent(stage, c - DEPTH[stage])

            send(stage, c)

        def all_sent(stage):
            def body(c, carry):
                waited = held[stage] & (c < chunks - DEPTH[stage]) if stage in held else False

                @pl.when(jnp.logical_not(waited))
                def _():
                    sent(stage, c)

                return carry

            lax.fori_loop(0, chunks, body, 0)

        def per_chunk(body):
            def step(c, carry):
                body(c, span(c))
                return carry

            lax.fori_loop(0, chunks, step, 0)

        def transpose(*which):
            for i in which:
                wts_t[i] = wts[i].T


        def normalize(wide, gain):
            inv = lax.rsqrt(jnp.mean(wide * wide, axis=-1, keepdims=True) + EPS)
            return inv, (wide * inv * gain).astype(jnp.bfloat16)

        lane, slab = lax.rem(me // (far // 4), 4), lax.rem(me // far, 4)
        held = {FAR_FWD: ((lane == 1) | (lane == 2)), FAR_BWD: ((lane == 1) | (lane == 2)) | (lax.rem(me, 2) == 1)}

        for one in gains + loads[:1]:
            one.wait()
        gain1 = g1_ref[...].reshape(1, C)
        gain2 = g2_ref[...].reshape(1, C)
        inv, normed = normalize(x_v[...].astype(jnp.float32), gain1)
        inv1[...] = inv
        nrm1[1] = normed
        pl.semaphore_wait(barrier, sum(exists(distance).astype(jnp.int32) for distance in partners))

        def first_send(c, at):
            send(NEAR_FWD, c)

        per_chunk(first_send)
        loads[1].wait()
        own[...] = dot(nrm1[1], wts[1])
        loads[2].wait()
        loads[3].wait()

        def first_forward(c, at):
            receive(NEAR_FWD, c)
            pre = own[at, :] + dot(nrm1[0, at], wts[0]) + dot(nrm1[2, at], wts[2])
            act, slope_pre1[at, :] = gelu_and_slope(pre)
            mid = dot(act.astype(jnp.bfloat16), wts[3])
            hid, slope_mid1[at, :] = gelu_and_slope(mid)
            result = x_v[at, :].astype(jnp.float32) + dot(hid.astype(jnp.bfloat16), wts[4])
            result = result.astype(jnp.bfloat16)
            x2[at, :] = result
            inv, normed = normalize(result.astype(jnp.float32), gain2)
            inv2[at, :] = inv
            nrm2[1, at] = normed
            send_far(FAR_FWD, c)

        per_chunk(first_forward)

        for i in (4, 5, 6, 7):
            loads[i].wait()
        transpose(9)
        ghid2[...] = dot(cot_v[...], wts_t[9])
        own[...] = dot(nrm2[1], wts[6])
        transpose(8)

        def second_block(c, at):
            receive(FAR_FWD, c)
            pre = own[at, :] + dot(nrm2[0, at], wts[5]) + dot(nrm2[2, at], wts[7])
            act, slope_pre = gelu_and_slope(pre)
            mid = dot(act.astype(jnp.bfloat16), wts[8])
            hid, slope_mid = gelu_and_slope(mid)
            hid2[at, :] = hid.astype(jnp.bfloat16)
            grad_mid = (ghid2[at, :] * slope_mid).astype(jnp.bfloat16)
            grad_act = dot(grad_mid, wts_t[8])
            gp2[1, at] = (grad_act * slope_pre).astype(jnp.bfloat16)
            send_far(FAR_BWD, c)

            @pl.when(c == 0)
            def _():
                transpose(5, 6, 7)

            @pl.when(c == 1)
            def _():
                transpose(4, 3)

            @pl.when(c == 2)
            def _():
                transpose(0, 1, 2)

        per_chunk(second_block)
        out_v[...] = (x2[...].astype(jnp.float32) + dot(hid2[...], wts[9])).astype(jnp.bfloat16)
        store_out = pltpu.make_async_copy(out_v, out_hbm, store_sem.at[0])
        store_out.start()
        own[...] = dot(gp2[1], wts_t[6])

        def norm_backward(dy, wide, inv, gain, grad_norm):
            scaled = gain * grad_norm
            inner = jnp.mean(wide * scaled, axis=-1, keepdims=True)
            return (dy + (inv * scaled - wide * (inv * inv * inv * inner))).astype(jnp.bfloat16)

        def second_to_first(c, at):
            receive(FAR_BWD, c)
            grad_norm = own[at, :] + dot(gp2[2, at], wts_t[5]) + dot(gp2[0, at], wts_t[7])
            dy = norm_backward(
                cot_v[at, :].astype(jnp.float32), x2[at, :].astype(jnp.float32), inv2[at, :], gain2, grad_norm
            )
            dy1[at, :] = dy
            grad_mid = (dot(dy, wts_t[4]) * slope_mid1[at, :]).astype(jnp.bfloat16)
            gp1[1, at] = (dot(grad_mid, wts_t[3]) * slope_pre1[at, :]).astype(jnp.bfloat16)
            send(NEAR_BWD, c)

        per_chunk(second_to_first)
        own[...] = dot(gp1[1], wts_t[1])

        def first_backward(c, at):
            receive(NEAR_BWD, c)
            grad_norm = own[at, :] + dot(gp1[2, at], wts_t[0]) + dot(gp1[0, at], wts_t[2])
            gin_v[at, :] = norm_backward(
                dy1[at, :].astype(jnp.float32), x_v[at, :].astype(jnp.float32), inv1[at, :], gain1, grad_norm
            )

        per_chunk(first_backward)
        store_gin = pltpu.make_async_copy(gin_v, gin_hbm, store_sem.at[1])
        store_gin.start()
        for stage in range(4):
            all_sent(stage)
        store_out.wait()
        store_gin.wait()

    return kernel


def solution(mesh):
    devices = mesh.shape["seq"]
    chunks = 4

    def per_device(x, g1, w1, m1, p1, g2, w2, m2, p2, cot):
        rows = x.shape[0]
        span = devices * rows
        near, far = 256 // rows, 4096 // rows
        assert span == 65536
        bf16 = lambda *lead: pltpu.VMEM((*lead, rows, C), jnp.bfloat16)
        f32 = lambda: pltpu.VMEM((rows, C), jnp.float32)
        whole = pl.BlockSpec(memory_space=pl.ANY)
        vmem = pl.BlockSpec(memory_space=pltpu.VMEM)
        block = jax.ShapeDtypeStruct((rows, C), jnp.bfloat16)
        results = pl.pallas_call(
            make_kernel(devices, near, far, rows, chunks),
            out_shape=(block, block),
            in_specs=[whole] * 10,
            out_specs=(whole, whole),
            scratch_shapes=[
                pltpu.VMEM((10, C, C), jnp.bfloat16),
                pltpu.VMEM((10, C, C), jnp.bfloat16),
                bf16(), bf16(), bf16(3), bf16(3), bf16(3), bf16(3), bf16(), bf16(), bf16(), bf16(), bf16(),
                f32(), f32(), f32(), f32(), f32(), f32(),
                pltpu.VMEM((rows, 1), jnp.float32),
                pltpu.VMEM((rows, 1), jnp.float32),
                pltpu.VMEM((C,), jnp.float32),
                pltpu.VMEM((C,), jnp.float32),
                pltpu.SemaphoreType.DMA((10,)),
                pltpu.SemaphoreType.DMA((2,)),
                pltpu.SemaphoreType.DMA((4, 2, chunks)),
                pltpu.SemaphoreType.DMA((4, 2, chunks)),
            ],
            compiler_params=pltpu.CompilerParams(
                collective_id=0, has_side_effects=True, vmem_limit_bytes=62 << 20
            ),
        )(x, g1, w1, m1, p1, g2, w2, m2, p2, cot)

        def hand_over(a, b, a_out, b_out):
            a_out[...] = a[...]
            b_out[...] = b[...]

        return pl.pallas_call(
            hand_over,
            out_shape=(block, block),
            in_specs=[vmem, vmem],
            out_specs=(vmem, vmem),
            compiler_params=pltpu.CompilerParams(vmem_limit_bytes=62 << 20),
        )(*results)

    return jax.shard_map(
        per_device,
        mesh=mesh,
        in_specs=(P("seq", None), P(), P(), P(), P(), P(), P(), P(), P(), P("seq", None)),
        out_specs=(P("seq", None), P("seq", None)),
        check_vma=False,
    )
```
